32 devices in a mesh: member: 2 (over core), space: 16 (over z, y, x).
Axes of the slice: x: 2, y: 2, z: 4, core: 2. Of those that a mesh axis runs over, the one named last changes fastest.
Arguments:
- background: bfloat16 [64, 256, 2560], P('member', 'space'), may hold values from -6 to 6
- obs_ens: bfloat16 [64, 20480], P('member', 'space'), may hold values from -6 to 6
- obs_value: bfloat16 [20480], P('space'), may hold values from -6 to 6
- obs_weight: bfloat16 [20480], P('space'), may hold values from 0.049804688 to 1
- obs_region: int32 [20480], P('space'), may hold values from 0 to 255, as said below
- region_order: int32 [256], replicated, may hold values from 0 to 255, each once
Outputs:
- analysis: bfloat16 [64, 256, 2560], P('member', 'space')
The draws below stay inside these ranges and needn't reach their ends.
Inputs may be any that keep to these rules, and one draw needn't show every extreme that they name: `obs_region`: in each aligned block of 1280 entries (the observations of one index of space) no region is named more than 32 times, and the same region is named exactly 32 times in every block. `region_order`: each region once.
All inputs are finite; a program needn't handle non-finite values.
Results may differ from the reference program's by a relative error of at most 0.0043.
Values may be sent and summed in bfloat16 or wider, within the bound.
A program may use at most 128 MiB of HBM per device.

```python
import math
import jax
import jax.numpy as jnp
from jax import lax

TRIAL_COUNT = 64
NS_ITERS = 4
F = 2560
REGIONS = 256
OBS_DEV = 1280
OBS = 20480
CAP = 32


def draw_obs_region(key, part):
    blocks = OBS // OBS_DEV
    busy_key, pull_key, block_key = jax.random.split(key, 3)
    busiest = jax.random.randint(busy_key, (), 0, REGIONS)
    popularity = jax.random.randint(pull_key, (REGIONS,), 3, 7)
    slot_count = REGIONS * CAP
    slot_region = jnp.arange(slot_count, dtype=jnp.int32) // CAP

    def one_block(sub_key):
        ranking_key, order_key = jax.random.split(sub_key)
        ranking = jax.random.randint(ranking_key, (slot_count,), 0, 1024) * popularity[slot_region]
        ranking = ranking * slot_count + jnp.arange(slot_count, dtype=jnp.int32)
        ranking = jnp.where(slot_region == busiest, -1, ranking)
        chosen = lax.top_k(ranking, OBS_DEV - CAP)[1]
        picked = jnp.concatenate([jnp.full((CAP,), busiest, jnp.int32), slot_region[chosen]])
        return picked[jax.random.permutation(order_key, OBS_DEV)]
    return jax.vmap(one_block)(jax.random.split(block_key, blocks)).reshape(OBS)


def shard_levels(stream_key, extent, cuts, least, top_value):
    gain, own = 1.0, jax.random.fold_in(stream_key, 6)
    for axis_at, shards_of in cuts:
        steps = jnp.exp(jax.random.uniform(jax.random.fold_in(own, axis_at), (shards_of,), jnp.float32, least / len(cuts), top_value / len(cuts)))
        gain = gain * jnp.repeat(steps, extent[axis_at] // shards_of).reshape([-1 if axis == axis_at else 1 for axis in range(len(extent))])
    return gain


def gaussian(key, extent, scale, most, cuts=(), kind=jnp.bfloat16):
    entries = scale * jax.random.normal(key, extent, jnp.float32)
    if cuts:
        entries = entries * shard_levels(key, extent, cuts, -0.22, 0.18)
    return jnp.clip(entries, -most, most).astype(kind)


def setup_inputs(seed: int = 0) -> dict:
    splits = jax.random.split(jax.random.key(seed), 7)
    background = gaussian(splits[0], (TRIAL_COUNT, REGIONS, F), 1.0, 6.0, ((0, 2), (1, 16)))
    obs_ens = gaussian(splits[1], (TRIAL_COUNT, OBS), 1.0, 6.0, ((0, 2), (1, 16)))
    obs_value = gaussian(splits[2], (OBS,), 1.0, 6.0, ((0, 16),))
    obs_weight = jnp.clip(jnp.exp(math.log(1.0) - 2.9996462 * jax.random.uniform(splits[3], (OBS,), jnp.float32) ** shard_levels(splits[3], (OBS,), ((0, 16),), -0.2, 0.2)), 0.049804688, 1.0).astype(jnp.bfloat16)
    obs_region = draw_obs_region(jax.random.fold_in(splits[6], 71), 0)
    region_order = jax.random.permutation(splits[5], REGIONS).astype(jnp.int32)
    return {"background": background, "obs_ens": obs_ens, "obs_value": obs_value, "obs_weight": obs_weight, "obs_region": obs_region, "region_order": region_order}


highest = lax.Precision.HIGHEST

def inverse_root(system):
    members = system.shape[-1]
    identity = jnp.eye(members, dtype=jnp.float32)
    frobenius = jnp.sqrt(lax.optimization_barrier(jnp.sum(system * system, axis=(1, 2))))
    direct_root = system / frobenius[:, None, None]
    inverse_part = jnp.broadcast_to(identity, system.shape)
    for iteration in range(NS_ITERS):
        correction = 1.5 * identity - 0.5 * jnp.matmul(inverse_part, direct_root, precision=highest)
        direct_root = jnp.matmul(direct_root, correction, precision=highest)
        inverse_part = jnp.matmul(correction, inverse_part, precision=highest)
    return (inverse_part, frobenius)

def transform_weights(gram_block, projection):
    members = gram_block.shape[-1]
    identity = jnp.eye(members, dtype=jnp.float32)
    system = (members - 1.0) * identity + gram_block
    inverse_part, frobenius = inverse_root(system)
    inner = jnp.matmul(inverse_part, projection[:, :, None], precision=highest)
    mean_shift = jnp.matmul(inverse_part, inner, precision=highest)[:, :, 0] / frobenius[:, None]
    dispersion_factor = jnp.sqrt((members - 1.0) / frobenius)
    return dispersion_factor[:, None, None] * inverse_part + mean_shift[:, :, None]

def reference(background, obs_ens, obs_value, obs_weight, obs_region, region_order):
    position = jnp.zeros((REGIONS,), jnp.int32).at[region_order].set(jnp.arange(REGIONS, dtype=jnp.int32))
    obs_pos = position[obs_region]
    ens_values = obs_ens.astype(jnp.float32)
    measured_average = lax.optimization_barrier(jnp.sum(ens_values, axis=0)) / TRIAL_COUNT
    trial_perturbation = ens_values - measured_average[None, :]
    departure = obs_value.astype(jnp.float32) - measured_average
    weight_values = obs_weight.astype(jnp.float32)
    anomaly_rows = trial_perturbation.T

    def per_region(index):
        local_weight = jnp.where(obs_pos == index, weight_values, jnp.float32(0.0))
        weighted = trial_perturbation * local_weight[None, :]
        gram_block = jnp.dot(weighted, anomaly_rows, precision=highest)
        projection = jnp.dot(weighted, departure, precision=highest)
        return (gram_block, projection)
    grams, projections = lax.map(per_region, jnp.arange(REGIONS, dtype=jnp.int32))
    weights = transform_weights(grams, projections).astype(jnp.bfloat16)
    weight_values_all = weights.astype(jnp.float32)
    state = background.astype(jnp.float32)
    combined = jnp.einsum('ipf,pij->jpf', state, weight_values_all)
    state_mean = lax.optimization_barrier(jnp.sum(state, axis=0)) / TRIAL_COUNT
    retained_fraction = 1.0 - lax.optimization_barrier(jnp.sum(weight_values_all, axis=1))
    return (combined + state_mean[None] * retained_fraction.T[:, :, None]).astype(jnp.bfloat16)
```

```python
import functools

import jax
import jax.numpy as jnp
from jax import lax
from jax.experimental import pallas as pl
from jax.experimental.pallas import tpu as pltpu
from jax.sharding import PartitionSpec as P

NS_ITERS = 4
CAP = 32
PAIR = 2
GROUPS = CAP // PAIR
MESH = pl.DeviceIdType.MESH
F32 = jnp.float32
BF16 = jnp.bfloat16


def iota(shape, axis):
    return lax.broadcasted_iota(jnp.int32, shape, axis)


def dot(a, b, dims=((1,), (0,))):
    return lax.dot_general(a, b, (dims, ((), ())), preferred_element_type=F32)


def split(a):
    high = a.astype(BF16)
    return high, (a - high.astype(F32)).astype(BF16)


def dot3(a, b):
    (ah, al), (bh, bl) = a, b
    return dot(ah, bh) + (dot(ah, bl) + dot(al, bh))


def weights_kernel(
    spaces, ens, value, weight, region, order, rowkey, background,
    wall, other_background,
    ens_other, spread, packed, arrived, wide, own_weights, other_weights,
    pair_send, pair_recv, route_send, route_recv,
):
    own, count = ens.shape
    members = 2 * own
    regions = order.shape[0] // spaces
    rows = regions * PAIR
    main = GROUPS * members
    m = lax.axis_index("member")
    me = lax.axis_index("space")
    partner = {"member": 1 - m}

    barrier = pltpu.get_barrier_semaphore()
    pl.semaphore_signal(barrier, inc=1, device_id=partner, device_id_type=MESH)

    def greet(step, carry):
        pl.semaphore_signal(
            barrier, inc=1, device_id={"space": lax.rem(me + step, spaces)}, device_id_type=MESH
        )
        return carry

    lax.fori_loop(1, spaces, greet, 0)
    pl.semaphore_wait(barrier, spaces)

    def pair_copy(src, dst, index):
        return pltpu.make_async_remote_copy(
            src_ref=src, dst_ref=dst, send_sem=pair_send.at[index], recv_sem=pair_recv.at[index],
            device_id=partner, device_id_type=MESH,
        )

    ens_copy = pair_copy(ens, ens_other, 0)
    ens_copy.start()
    state_copy = pair_copy(background, other_background, 1)
    state_copy.start()

    block = 256
    upper = jnp.where(iota((block, block), 0) < iota((block, block), 1), 1.0, 0.0).astype(BF16)
    offset = jnp.zeros((order.shape[0], 1), F32)
    ranks = []
    for at in range(0, count, block):
        hit = jnp.where(order[...] == region[:, at : at + block], 1.0, 0.0)
        earlier = dot(hit.astype(BF16), upper) + offset
        ranks.append(jnp.sum(hit * earlier, axis=0, keepdims=True))
        offset = offset + jnp.sum(hit, axis=1, keepdims=True)
    rank = jnp.concatenate(ranks, axis=1).astype(jnp.int32)
    group = rank // PAIR
    key = region[...] * PAIR + rank % PAIR
    picks = jnp.where(rowkey[...] == key, 1.0, 0.0).astype(BF16)

    ens_copy.wait()
    here, there = ens[...].astype(F32), ens_other[...].astype(F32)
    mean = (jnp.sum(here, axis=0, keepdims=True) + jnp.sum(there, axis=0, keepdims=True)) / members
    root = jnp.sqrt(weight[...].astype(F32))
    here = ((here - mean) * root).astype(BF16)
    there = ((there - mean) * root).astype(BF16)
    departure = (value[...].astype(F32) - mean) * root
    for g in range(GROUPS):
        mask = jnp.where(group == g, 1.0, 0.0).astype(BF16)
        spread[pl.ds(pl.multiple_of(g * members + m * own, own), own), :] = here * mask
        spread[pl.ds(pl.multiple_of(g * members + (1 - m) * own, own), own), :] = there * mask
    spread[main:, :] = jnp.where(iota((128, count), 0) == group, departure, 0.0).astype(BF16)
    packed[...] = dot(picks, spread[...], ((1,), (1,))).astype(BF16)

    def place(index):
        return pl.ds(pl.multiple_of(index * rows, rows), rows)

    def route(dest, source, landing):
        return pltpu.make_async_remote_copy(
            src_ref=packed.at[place(dest)], dst_ref=arrived.at[place(landing)],
            send_sem=route_send.at[dest], recv_sem=route_recv.at[source],
            device_id={"space": dest}, device_id_type=MESH,
        )

    def send(step, carry):
        route(lax.rem(me + step, spaces), me, me).start()
        return carry

    def receive(step, carry):
        source = lax.rem(me + spaces - step, spaces)
        route(lax.rem(me + step, spaces), source, source).wait()
        return carry

    lax.fori_loop(1, spaces, send, 0)
    arrived[place(me), :] = packed[place(me), :]
    lax.fori_loop(1, spaces, receive, 0)
    for j in range(wide.shape[0]):
        wide[j] = arrived[:, j * 128 : (j + 1) * 128].astype(F32)

    eye = jnp.where(iota((members, members), 0) == iota((members, members), 1), 1.0, 0.0)
    lane = iota((spaces, 128), 1)
    fold = (iota((128, 2 * members), 0) % 2 == 0) == (iota((128, 2 * members), 1) < members)
    systems, projections, norms = [], [], []
    for r in range(regions):
        at = [pl.ds(r * PAIR + k, spaces, stride=rows) for k in range(PAIR)]
        extra = [wide[GROUPS // 2, a, :] for a in at]
        left, right = [], []
        for j in range(GROUPS // 2):
            for k in range(PAIR):
                left.append(wide[j, at[k], :])
                right.append(jnp.where(lane // 2 == j, extra[k], 0.0))
        anomalies = jnp.concatenate(left, axis=0).astype(BF16)
        departures = jnp.concatenate(right, axis=0).astype(BF16)
        gram = dot(anomalies, anomalies, ((0,), (0,)))
        product = dot(departures, anomalies, ((0,), (0,)))
        product = jnp.sum(jnp.where(fold, product, 0.0), axis=0, keepdims=True)
        projections.append(product[:, :members] + product[:, members:])
        system = (members - 1.0) * eye + (gram[:members, :members] + gram[members:, members:])
        norm = jnp.sum(jnp.sum(system * system, axis=0, keepdims=True), axis=1, keepdims=True)
        norm = jnp.sqrt(norm)
        norms.append(norm)
        systems.append(system / norm)

    direct = systems
    direct_parts = [split(a) for a in direct]
    correction = [1.5 * eye - 0.5 * a for a in direct]
    inverse = correction
    inverse_parts = [split(a) for a in inverse]
    direct = [dot3(a, c) for a, c in zip(direct_parts, inverse_parts)]
    for iteration in range(1, NS_ITERS):
        direct_parts = [split(a) for a in direct]
        correction = [1.5 * eye - 0.5 * dot3(b, a) for a, b in zip(direct_parts, inverse_parts)]
        correction_parts = [split(a) for a in correction]
        inverse = [dot3(c, b) for c, b in zip(correction_parts, inverse_parts)]
        if iteration < NS_ITERS - 1:
            direct = [dot3(a, c) for a, c in zip(direct_parts, correction_parts)]
            inverse_parts = [split(a) for a in inverse]

    for r in range(regions):
        root_part, norm = inverse[r], norms[r]
        inner = jnp.sum(root_part * projections[r], axis=1, keepdims=True)
        shift = jnp.sum(root_part * inner, axis=0, keepdims=True) / norm
        own_weights[r] = (jnp.sqrt((members - 1.0) / norm) * root_part + shift).astype(BF16)

    mine = pl.ds(pl.multiple_of(m * own, own), own)
    theirs = pl.ds(pl.multiple_of((1 - m) * own, own), own)
    weight_copy = pair_copy(own_weights.at[:, theirs, :], other_weights, 2)
    weight_copy.start()
    wall[m] = own_weights[:, mine, :]
    weight_copy.wait()
    wall[1 - m] = other_weights[...]
    state_copy.wait()


def analysis_kernel(weights, here, there, out, wide, retained):
    own, regions, tile = here.shape
    members = 2 * own
    half = own * regions
    m = lax.axis_index("member")

    @pl.when(pl.program_id(0) == 0)
    def expand():
        row, col = iota((half, half), 0), iota((half, half), 1)
        order = jnp.where(col == (row % regions) * own + row // regions, 1.0, 0.0).astype(BF16)
        columns = dot(order, weights[...])
        retained[...] = 1.0 - jnp.sum(columns, axis=1, keepdims=True)
        i, c = iota((members, 2 * half), 0), iota((members, 2 * half), 1)
        copies = jnp.where((c // regions + m * own) % members == i, 1.0, 0.0).astype(BF16)
        full = dot(columns.astype(BF16), copies)
        row, col = iota((half, 2 * half), 0), iota((half, 2 * half), 1)
        wide[:half] = jnp.where(row % regions == col % regions, full, 0.0).astype(BF16)
        row, col = iota((regions, 2 * half), 0), iota((regions, 2 * half), 1)
        wide[half:] = jnp.where(row == col % regions, 1.0 / members, 0.0).astype(BF16)

    total = dot(wide[:, :half], here[...].reshape(half, tile))
    total += dot(wide[:, half:], there[...].reshape(half, tile))
    state_mean = total[half:]
    combined = total[:half].reshape(own, regions, tile)
    share = retained[...].reshape(own, regions, 1)
    out[...] = (combined + share * state_mean[None]).astype(BF16)


def shards(spaces, background, obs_ens, obs_value, obs_weight, obs_region, region_order):
    own, own_regions, width = background.shape
    count = obs_ens.shape[1]
    regions = own_regions // 2
    members = 2 * own
    m = lax.axis_index("member")
    order = region_order.reshape(spaces, 2, regions)
    order = jnp.where(m == 0, order[:, 0], order[:, 1]).reshape(spaces * regions, 1)
    rowkey = (order * PAIR + jnp.arange(PAIR, dtype=jnp.int32)[None]).reshape(-1, 1)
    rows = regions * PAIR
    lanes = GROUPS * members + 128
    vmem = pl.BlockSpec(memory_space=pltpu.VMEM)
    hbm = pl.BlockSpec(memory_space=pl.ANY)
    weights, other = pl.pallas_call(
        functools.partial(weights_kernel, spaces),
        out_shape=(
            jax.ShapeDtypeStruct((2, regions, own, members), BF16),
            jax.ShapeDtypeStruct(background.shape, BF16),
        ),
        in_specs=[vmem] * 6 + [hbm],
        out_specs=(vmem, hbm),
        scratch_shapes=[
            pltpu.VMEM((own, count), BF16),
            pltpu.VMEM((lanes, count), BF16),
            pltpu.VMEM((spaces * rows, lanes), BF16),
            pltpu.VMEM((spaces * rows, lanes), BF16),
            pltpu.VMEM((lanes // 128, spaces * rows, 128), F32),
            pltpu.VMEM((regions, members, members), BF16),
            pltpu.VMEM((regions, own, members), BF16),
            pltpu.SemaphoreType.DMA((3,)),
            pltpu.SemaphoreType.DMA((3,)),
            pltpu.SemaphoreType.DMA((spaces,)),
            pltpu.SemaphoreType.DMA((spaces,)),
        ],
        compiler_params=pltpu.CompilerParams(
            collective_id=0, has_side_effects=True, vmem_limit_bytes=56 * 2**20
        ),
        name="region_weights",
    )(
        obs_ens, obs_value.reshape(1, count), obs_weight.reshape(1, count),
        obs_region.reshape(1, count), order, rowkey, background,
    )
    tile = 512
    half = own * own_regions
    block = pl.BlockSpec((own, own_regions, tile), lambda f: (0, 0, f))
    return pl.pallas_call(
        analysis_kernel,
        out_shape=jax.ShapeDtypeStruct(background.shape, BF16),
        grid=(width // tile,),
        in_specs=[pl.BlockSpec((half, members), lambda f: (0, 0)), block, block],
        out_specs=block,
        scratch_shapes=[
            pltpu.VMEM((half + own_regions, 2 * half), BF16),
            pltpu.VMEM((half, 1), F32),
        ],
        compiler_params=pltpu.CompilerParams(vmem_limit_bytes=40 * 2**20),
        name="analysis",
    )(weights.reshape(half, members), background, other)


def solution(mesh):
    return jax.shard_map(
        functools.partial(shards, mesh.shape["space"]),
        mesh=mesh,
        in_specs=(
            P("member", "space", None),
            P("member", "space"),
            P("space"),
            P("space"),
            P("space"),
            P(),
        ),
        out_specs=P("member", "space", None),
        check_vma=False,
    )
```

```python
import functools

import jax
import jax.numpy as jnp
from jax import lax
from jax.experimental import pallas as pl
from jax.experimental.pallas import tpu as pltpu
from jax.sharding import PartitionSpec as P

NS_ITERS = 4
CAP = 32
PAIR = 2
GROUPS = CAP // PAIR
MESH = pl.DeviceIdType.MESH
F32 = jnp.float32
BF16 = jnp.bfloat16


def iota(shape, axis):
    return lax.broadcasted_iota(jnp.int32, shape, axis)


def dot(a, b, dims=((1,), (0,))):
    return lax.dot_general(a, b, (dims, ((), ())), preferred_element_type=F32)


def split(a):
    high = a.astype(BF16)
    return high, (a - high.astype(F32)).astype(BF16)


def dot3(a, b):
    (ah, al), (bh, bl) = a, b
    return dot(ah, bh) + (dot(ah, bl) + dot(al, bh))


def weights_kernel(
    spaces, ens, value, weight, region, region_order, background,
    wall, other_background,
    ens_other, spread, packed, arrived, wide, own_weights, other_weights,
    pair_send, pair_recv, route_send, route_recv,
):
    own, count = ens.shape
    members = 2 * own
    total = region_order.shape[0]
    regions = total // spaces // 2
    rows = regions * PAIR
    m = lax.axis_index("member")
    me = lax.axis_index("space")
    partner = {"member": 1 - m}

    barrier = pltpu.get_barrier_semaphore()
    pl.semaphore_signal(barrier, inc=1, device_id=partner, device_id_type=MESH)

    def greet(step, carry):
        pl.semaphore_signal(
            barrier, inc=1, device_id={"space": lax.rem(me + step, spaces)}, device_id_type=MESH
        )
        return carry

    lax.fori_loop(1, spaces, greet, 0)
    pl.semaphore_wait(barrier, spaces)

    def pair_copy(src, dst, index):
        return pltpu.make_async_remote_copy(
            src_ref=src, dst_ref=dst, send_sem=pair_send.at[index], recv_sem=pair_recv.at[index],
            device_id=partner, device_id_type=MESH,
        )

    ens_copy = pair_copy(ens, ens_other, 0)
    ens_copy.start()
    state_copy = pair_copy(background, other_background, 1)
    state_copy.start()

    def column(height, per_space, per_region):
        row, col = iota((height, 1), 0), iota((1, total), 1)
        at = row // per_space * (2 * regions) + m * regions + row % per_space // per_region
        held = region_order[...].reshape(1, total).astype(F32)
        picked = jnp.sum(jnp.where(col == at, held, 0.0), axis=1, keepdims=True)
        return picked.astype(jnp.int32)

    order = column(spaces * regions, regions, 1)
    rowkey = column(spaces * rows, rows, PAIR) * PAIR + iota((spaces * rows, 1), 0) % PAIR
    region_row = region[...].reshape(1, count)
    root = jnp.sqrt(weight[...].reshape(1, count).astype(F32))

    block = 256
    upper = jnp.where(iota((block, block), 0) < iota((block, block), 1), 1.0, 0.0).astype(BF16)
    offset = jnp.zeros((spaces * regions, 1), F32)
    ranks = []
    for at in range(0, count, block):
        hit = jnp.where(order == region_row[:, at : at + block], 1.0, 0.0)
        earlier = dot(hit.astype(BF16), upper) + offset
        ranks.append(jnp.sum(hit * earlier, axis=0, keepdims=True))
        offset = offset + jnp.sum(hit, axis=1, keepdims=True)
    rank = jnp.concatenate(ranks, axis=1).astype(jnp.int32)
    group = rank // PAIR
    key = region_row * PAIR + rank % PAIR
    picks = jnp.where(rowkey == key, 1.0, 0.0).astype(BF16)

    ens_copy.wait()
    here, there = ens[...].astype(F32), ens_other[...].astype(F32)
    mean = (jnp.sum(here, axis=0, keepdims=True) + jnp.sum(there, axis=0, keepdims=True)) / members
    here = (here - mean) * root
    there = (there - mean) * root
    departure = (value[...].reshape(1, count).astype(F32) - mean) * root
    last = jnp.where(m == 0, there[own - 1 :], here[own - 1 :])
    lift = last / (jnp.sqrt(F32(members)) - 1.0)
    final = iota((own, 1), 0) == own - 1
    here = jnp.where(final & (m == 1), departure, here + lift).astype(BF16)
    there = jnp.where(final & (m == 0), departure, there + lift).astype(BF16)
    for g in range(GROUPS):
        mask = jnp.where(group == g, 1.0, 0.0).astype(BF16)
        spread[pl.ds(pl.multiple_of(g * members + m * own, own), own), :] = here * mask
        spread[pl.ds(pl.multiple_of(g * members + (1 - m) * own, own), own), :] = there * mask
    packed[...] = dot(picks, spread[...], ((1,), (1,))).astype(BF16)

    def place(index):
        return pl.ds(pl.multiple_of(index * rows, rows), rows)

    def route(dest, source, landing):
        return pltpu.make_async_remote_copy(
            src_ref=packed.at[place(dest)], dst_ref=arrived.at[place(landing)],
            send_sem=route_send.at[dest], recv_sem=route_recv.at[source],
            device_id={"space": dest}, device_id_type=MESH,
        )

    def send(step, carry):
        route(lax.rem(me + step, spaces), me, me).start()
        return carry

    def receive(step, carry):
        source = lax.rem(me + spaces - step, spaces)
        route(lax.rem(me + step, spaces), source, source).wait()
        return carry

    lax.fori_loop(1, spaces, send, 0)
    arrived[place(me), :] = packed[place(me), :]
    lax.fori_loop(1, spaces, receive, 0)
    for j in range(wide.shape[0]):
        wide[j] = arrived[:, j * 128 : (j + 1) * 128].astype(F32)

    eye = jnp.where(iota((members, members), 0) == iota((members, members), 1), 1.0, 0.0)
    edge = jnp.sqrt(F32(members))
    kept_row, kept_col = iota((1, members), 1) < members - 1, iota((members, 1), 0) < members - 1
    mirror_row = jnp.where(kept_row, 1.0, 1.0 - edge)
    mirror_col = jnp.where(kept_col, 1.0, 1.0 - edge)
    scale = 1.0 / (members - edge)
    systems, projections, norms = [], [], []
    for r in range(regions):
        at = [pl.ds(r * PAIR + k, spaces, stride=rows) for k in range(PAIR)]
        left = [wide[j, at[k], :] for j in range(GROUPS // 2) for k in range(PAIR)]
        anomalies = jnp.concatenate(left, axis=0).astype(BF16)
        gram = dot(anomalies, anomalies, ((0,), (0,)))
        gram = gram[:members, :members] + gram[members:, members:]
        projection = jnp.where(kept_row, gram[members - 1 :], 0.0)
        gram = jnp.where(kept_row & kept_col, gram, 0.0)
        reflected = jnp.sum(projection, axis=1, keepdims=True) * scale
        projections.append(projection - reflected * mirror_row)
        gram = gram - mirror_col * (jnp.sum(gram, axis=0, keepdims=True) * scale)
        gram = gram - (jnp.sum(gram, axis=1, keepdims=True) * scale) * mirror_row
        system = (members - 1.0) * eye + gram
        norm = jnp.sum(jnp.sum(system * system, axis=0, keepdims=True), axis=1, keepdims=True)
        norm = jnp.sqrt(norm)
        norms.append(norm)
        systems.append(system / norm)

    direct = systems
    direct_parts = [split(a) for a in direct]
    correction = [1.5 * eye - 0.5 * a for a in direct]
    inverse = correction
    inverse_parts = [split(a) for a in inverse]
    direct = [dot3(a, c) for a, c in zip(direct_parts, inverse_parts)]
    for iteration in range(1, NS_ITERS):
        direct_parts = [split(a) for a in direct]
        correction = [1.5 * eye - 0.5 * dot3(b, a) for a, b in zip(direct_parts, inverse_parts)]
        correction_parts = [split(a) for a in correction]
        inverse = [dot3(c, b) for c, b in zip(correction_parts, inverse_parts)]
        if iteration < NS_ITERS - 1:
            direct = [dot3(a, c) for a, c in zip(direct_parts, correction_parts)]
            inverse_parts = [split(a) for a in inverse]

    for r in range(regions):
        root_part, norm = inverse[r], norms[r]
        inner = jnp.sum(root_part * projections[r], axis=1, keepdims=True)
        shift = jnp.sum(root_part * inner, axis=0, keepdims=True) / norm
        own_weights[r] = (jnp.sqrt((members - 1.0) / norm) * root_part + shift).astype(BF16)

    mine = pl.ds(pl.multiple_of(m * own, own), own)
    theirs = pl.ds(pl.multiple_of((1 - m) * own, own), own)
    weight_copy = pair_copy(own_weights.at[:, theirs, :], other_weights, 2)
    weight_copy.start()
    wall[m] = own_weights[:, mine, :]
    weight_copy.wait()
    wall[1 - m] = other_weights[...]
    state_copy.wait()


def analysis_kernel(weights, here, there, out, wide, retained):
    own, regions, tile = here.shape
    members = 2 * own
    half = own * regions
    m = lax.axis_index("member")

    @pl.when(pl.program_id(0) == 0)
    def expand():
        row = iota((half, 1), 0)
        region = row % regions
        order = jnp.where(iota((1, half), 1) == region * own + row // regions, 1.0, 0.0)
        order = order.astype(BF16)
        columns = dot(order, weights[...])
        retained[...] = 1.0 - jnp.sum(columns, axis=1, keepdims=True)
        c = iota((1, 2 * half), 1)
        member, lane_region = (c // regions + m * own) % members, c % regions
        copies = jnp.where(member == iota((members, 1), 0), 1.0, 0.0).astype(BF16)
        full = dot(columns.astype(BF16), copies)
        wide[:half] = jnp.where(region == lane_region, full, 0.0).astype(BF16)
        same = iota((regions, 1), 0) == lane_region
        wide[half:] = jnp.where(same, 1.0 / members, 0.0).astype(BF16)

    total = dot(wide[:, :half], here[...].reshape(half, tile))
    total += dot(wide[:, half:], there[...].reshape(half, tile))
    state_mean = total[half:]
    combined = total[:half].reshape(own, regions, tile)
    share = retained[...].reshape(own, regions, 1)
    out[...] = (combined + share * state_mean[None]).astype(BF16)


def shards(spaces, background, obs_ens, obs_value, obs_weight, obs_region, region_order):
    own, own_regions, width = background.shape
    count = obs_ens.shape[1]
    regions = own_regions // 2
    members = 2 * own
    rows = regions * PAIR
    lanes = GROUPS * members
    vmem = pl.BlockSpec(memory_space=pltpu.VMEM)
    hbm = pl.BlockSpec(memory_space=pl.ANY)
    weights, other = pl.pallas_call(
        functools.partial(weights_kernel, spaces),
        out_shape=(
            jax.ShapeDtypeStruct((2, regions, own, members), BF16),
            jax.ShapeDtypeStruct(background.shape, BF16),
        ),
        in_specs=[vmem] * 5 + [hbm],
        out_specs=(vmem, hbm),
        scratch_shapes=[
            pltpu.VMEM((own, count), BF16),
            pltpu.VMEM((lanes, count), BF16),
            pltpu.VMEM((spaces * rows, lanes), BF16),
            pltpu.VMEM((spaces * rows, lanes), BF16),
            pltpu.VMEM((lanes // 128, spaces * rows, 128), F32),
            pltpu.VMEM((regions, members, members), BF16),
            pltpu.VMEM((regions, own, members), BF16),
            pltpu.SemaphoreType.DMA((3,)),
            pltpu.SemaphoreType.DMA((3,)),
            pltpu.SemaphoreType.DMA((spaces,)),
            pltpu.SemaphoreType.DMA((spaces,)),
        ],
        compiler_params=pltpu.CompilerParams(
            collective_id=0, has_side_effects=True, vmem_limit_bytes=56 * 2**20
        ),
        name="region_weights",
    )(
        obs_ens, obs_value, obs_weight, obs_region, region_order, background,
    )
    tile = 512
    half = own * own_regions
    block = pl.BlockSpec((own, own_regions, tile), lambda f: (0, 0, f))
    return pl.pallas_call(
        analysis_kernel,
        out_shape=jax.ShapeDtypeStruct(background.shape, BF16),
        grid=(width // tile,),
        in_specs=[pl.BlockSpec((half, members), lambda f: (0, 0)), block, block],
        out_specs=block,
        scratch_shapes=[
            pltpu.VMEM((half + own_regions, 2 * half), BF16),
            pltpu.VMEM((half, 1), F32),
        ],
        compiler_params=pltpu.CompilerParams(vmem_limit_bytes=60 * 2**20),
        name="analysis",
    )(weights.reshape(half, members), background, other)


def solution(mesh):
    return jax.shard_map(
        functools.partial(shards, mesh.shape["space"]),
        mesh=mesh,
        in_specs=(
            P("member", "space", None),
            P("member", "space"),
            P("space"),
            P("space"),
            P("space"),
            P(),
        ),
        out_specs=P("member", "space", None),
        check_vma=False,
    )
```

```python
import functools

import jax
import jax.numpy as jnp
from jax import lax
from jax.experimental import pallas as pl
from jax.experimental.pallas import tpu as pltpu
from jax.sharding import PartitionSpec as P

NS_ITERS = 4
CAP = 32
PAIR = 2
GROUPS = CAP // PAIR
CHUNKS = 2
TILE = 512
MESH = pl.DeviceIdType.MESH
F32 = jnp.float32
BF16 = jnp.bfloat16


def iota(shape, axis):
    return lax.broadcasted_iota(jnp.int32, shape, axis)


def dot(a, b, dims=((1,), (0,))):
    return lax.dot_general(a, b, (dims, ((), ())), preferred_element_type=F32)


def split(a):
    high = a.astype(BF16)
    return high, (a - high.astype(F32)).astype(BF16)


def dot3(a, b):
    (ah, al), (bh, bl) = a, b
    return dot(ah, bh) + (dot(ah, bl) + dot(al, bh))


def weights_kernel(
    spaces, ens, value, weight, region, region_order, background,
    wall, other_background,
    ens_other, spread, packed, arrived, wide, own_weights, other_weights,
    pair_send, pair_recv, route_send, route_recv,
):
    own, count = ens.shape
    members = 2 * own
    total = region_order.shape[0]
    regions = total // spaces // 2
    rows = regions * PAIR
    m = lax.axis_index("member")
    me = lax.axis_index("space")
    partner = {"member": 1 - m}

    barrier = pltpu.get_barrier_semaphore()
    pl.semaphore_signal(barrier, inc=1, device_id=partner, device_id_type=MESH)

    def greet(step, carry):
        pl.semaphore_signal(
            barrier, inc=1, device_id={"space": lax.rem(me + step, spaces)}, device_id_type=MESH
        )
        return carry

    lax.fori_loop(1, spaces, greet, 0)
    pl.semaphore_wait(barrier, spaces)

    def pair_copy(src, dst, index):
        return pltpu.make_async_remote_copy(
            src_ref=src, dst_ref=dst, send_sem=pair_send.at[index], recv_sem=pair_recv.at[index],
            device_id=partner, device_id_type=MESH,
        )

    ens_copy = pair_copy(ens, ens_other, 0)
    ens_copy.start()
    state_copy = pair_copy(background, other_background, 1)
    state_copy.start()

    def column(height, per_space, per_region):
        row, col = iota((height, 1), 0), iota((1, total), 1)
        at = row // per_space * (2 * regions) + m * regions + row % per_space // per_region
        held = region_order[...].reshape(1, total).astype(F32)
        picked = jnp.sum(jnp.where(col == at, held, 0.0), axis=1, keepdims=True)
        return picked.astype(jnp.int32)

    order = column(spaces * regions, regions, 1)
    rowkey = column(spaces * rows, rows, PAIR) * PAIR + iota((spaces * rows, 1), 0) % PAIR
    region_row = region[...].reshape(1, count)
    root = jnp.sqrt(weight[...].reshape(1, count).astype(F32))

    block = 256
    upper = jnp.where(iota((block, block), 0) < iota((block, block), 1), 1.0, 0.0).astype(BF16)
    offset = jnp.zeros((spaces * regions, 1), F32)
    ranks = []
    for at in range(0, count, block):
        hit = jnp.where(order == region_row[:, at : at + block], 1.0, 0.0)
        earlier = dot(hit.astype(BF16), upper) + offset
        ranks.append(jnp.sum(hit * earlier, axis=0, keepdims=True))
        offset = offset + jnp.sum(hit, axis=1, keepdims=True)
    rank = jnp.concatenate(ranks, axis=1).astype(jnp.int32)
    group = rank // PAIR
    key = region_row * PAIR + rank % PAIR
    picks = jnp.where(rowkey == key, 1.0, 0.0).astype(BF16)

    ens_copy.wait()
    here, there = ens[...].astype(F32), ens_other[...].astype(F32)
    mean = (jnp.sum(here, axis=0, keepdims=True) + jnp.sum(there, axis=0, keepdims=True)) / members
    here = (here - mean) * root
    there = (there - mean) * root
    departure = (value[...].reshape(1, count).astype(F32) - mean) * root
    last = jnp.where(m == 0, there[own - 1 :], here[own - 1 :])
    lift = last / (jnp.sqrt(F32(members)) - 1.0)
    final = iota((own, 1), 0) == own - 1
    here = jnp.where(final & (m == 1), departure, here + lift).astype(BF16)
    there = jnp.where(final & (m == 0), departure, there + lift).astype(BF16)
    def place(index):
        return pl.ds(pl.multiple_of(index * rows, rows), rows)

    def route(chunk, dest, source, landing):
        return pltpu.make_async_remote_copy(
            src_ref=packed.at[chunk, place(dest)], dst_ref=arrived.at[chunk, place(landing)],
            send_sem=route_send.at[chunk, dest], recv_sem=route_recv.at[chunk, source],
            device_id={"space": dest}, device_id_type=MESH,
        )

    span = GROUPS // CHUNKS
    for chunk in range(CHUNKS):
        for g in range(span):
            mask = jnp.where(group == chunk * span + g, 1.0, 0.0).astype(BF16)
            spread[pl.ds(pl.multiple_of(g * members + m * own, own), own), :] = here * mask
            spread[pl.ds(pl.multiple_of(g * members + (1 - m) * own, own), own), :] = there * mask
        packed[chunk] = dot(picks, spread[...], ((1,), (1,))).astype(BF16)

        def send(step, carry):
            route(chunk, lax.rem(me + step, spaces), me, me).start()
            return carry

        lax.fori_loop(1, spaces, send, 0)

    tiles = wide.shape[0] // CHUNKS
    for chunk in range(CHUNKS):

        def receive(step, carry):
            source = lax.rem(me + spaces - step, spaces)
            route(chunk, lax.rem(me + step, spaces), source, source).wait()
            return carry

        arrived[chunk, place(me), :] = packed[chunk, place(me), :]
        lax.fori_loop(1, spaces, receive, 0)
        for j in range(tiles):
            wide[chunk * tiles + j] = arrived[chunk, :, j * 128 : (j + 1) * 128].astype(F32)

    eye = jnp.where(iota((members, members), 0) == iota((members, members), 1), 1.0, 0.0)
    edge = jnp.sqrt(F32(members))
    kept_row, kept_col = iota((1, members), 1) < members - 1, iota((members, 1), 0) < members - 1
    mirror_row = jnp.where(kept_row, 1.0, 1.0 - edge)
    mirror_col = jnp.where(kept_col, 1.0, 1.0 - edge)
    scale = 1.0 / (members - edge)
    systems, projections, norms = [], [], []
    for r in range(regions):
        at = [pl.ds(r * PAIR + k, spaces, stride=rows) for k in range(PAIR)]
        left = [wide[j, at[k], :] for j in range(GROUPS // 2) for k in range(PAIR)]
        anomalies = jnp.concatenate(left, axis=0).astype(BF16)
        gram = dot(anomalies, anomalies, ((0,), (0,)))
        gram = gram[:members, :members] + gram[members:, members:]
        projection = jnp.where(kept_row, gram[members - 1 :], 0.0)
        gram = jnp.where(kept_row & kept_col, gram, 0.0)
        reflected = jnp.sum(projection, axis=1, keepdims=True) * scale
        projections.append(projection - reflected * mirror_row)
        gram = gram - mirror_col * (jnp.sum(gram, axis=0, keepdims=True) * scale)
        gram = gram - (jnp.sum(gram, axis=1, keepdims=True) * scale) * mirror_row
        system = (members - 1.0) * eye + gram
        norm = jnp.sum(jnp.sum(system * system, axis=0, keepdims=True), axis=1, keepdims=True)
        norm = jnp.sqrt(norm)
        norms.append(norm)
        systems.append(system / norm)

    direct = systems
    direct_parts = [split(a) for a in direct]
    correction = [1.5 * eye - 0.5 * a for a in direct]
    inverse = correction
    inverse_parts = [split(a) for a in inverse]
    direct = [dot3(a, c) for a, c in zip(direct_parts, inverse_parts)]
    for iteration in range(1, NS_ITERS):
        direct_parts = [split(a) for a in direct]
        correction = [1.5 * eye - 0.5 * dot3(b, a) for a, b in zip(direct_parts, inverse_parts)]
        correction_parts = [split(a) for a in correction]
        inverse = [dot3(c, b) for c, b in zip(correction_parts, inverse_parts)]
        if iteration < NS_ITERS - 1:
            direct = [dot3(a, c) for a, c in zip(direct_parts, correction_parts)]
            inverse_parts = [split(a) for a in inverse]

    for r in range(regions):
        root_part, norm = inverse[r], norms[r]
        inner = jnp.sum(root_part * projections[r], axis=1, keepdims=True)
        shift = jnp.sum(root_part * inner, axis=0, keepdims=True) / norm
        own_weights[r] = (jnp.sqrt((members - 1.0) / norm) * root_part + shift).astype(BF16)

    mine = pl.ds(pl.multiple_of(m * own, own), own)
    theirs = pl.ds(pl.multiple_of((1 - m) * own, own), own)
    weight_copy = pair_copy(own_weights.at[:, theirs, :], other_weights, 2)
    weight_copy.start()
    wall[m] = own_weights[:, mine, :]
    weight_copy.wait()
    wall[1 - m] = other_weights[...]
    state_copy.wait()


def analysis_kernel(
    weights, here_any, there_any, out_any, here, there, out, wide, retained, sems
):
    own, regions, width = here.shape
    members = 2 * own
    half = own * regions
    tile = TILE
    m = lax.axis_index("member")
    steps = [pl.ds(at, tile) for at in range(0, width, tile)]

    def copy(kind, index):
        source, target = ((here_any, here), (there_any, there), (out, out_any))[kind]
        cut = steps[index]
        return pltpu.make_async_copy(
            source.at[:, :, cut], target.at[:, :, cut], sems.at[kind, index]
        )

    for index in range(len(steps)):
        copy(0, index).start()
        copy(1, index).start()

    row = iota((half, 1), 0)
    region = row % regions
    order = jnp.where(iota((1, half), 1) == region * own + row // regions, 1.0, 0.0)
    order = order.astype(BF16)
    columns = dot(order, weights[...])
    retained[...] = 1.0 - jnp.sum(columns, axis=1, keepdims=True)
    c = iota((1, 2 * half), 1)
    member, lane_region = (c // regions + m * own) % members, c % regions
    copies = jnp.where(member == iota((members, 1), 0), 1.0, 0.0).astype(BF16)
    full = dot(columns.astype(BF16), copies)
    wide[:half] = jnp.where(region == lane_region, full, 0.0).astype(BF16)
    same = iota((regions, 1), 0) == lane_region
    wide[half:] = jnp.where(same, 1.0 / members, 0.0).astype(BF16)

    for index, cut in enumerate(steps):
        copy(0, index).wait()
        copy(1, index).wait()
        total = dot(wide[:, :half], here[:, :, cut].reshape(half, tile))
        total += dot(wide[:, half:], there[:, :, cut].reshape(half, tile))
        combined = total[:half].reshape(own, regions, tile)
        share = retained[...].reshape(own, regions, 1)
        out[:, :, cut] = (combined + share * total[half:][None]).astype(BF16)
        copy(2, index).start()
    for index in range(len(steps)):
        copy(2, index).wait()


def shards(spaces, background, obs_ens, obs_value, obs_weight, obs_region, region_order):
    own, own_regions, width = background.shape
    count = obs_ens.shape[1]
    regions = own_regions // 2
    members = 2 * own
    rows = regions * PAIR
    lanes = GROUPS * members
    vmem = pl.BlockSpec(memory_space=pltpu.VMEM)
    hbm = pl.BlockSpec(memory_space=pl.ANY)
    weights, other = pl.pallas_call(
        functools.partial(weights_kernel, spaces),
        out_shape=(
            jax.ShapeDtypeStruct((2, regions, own, members), BF16),
            jax.ShapeDtypeStruct(background.shape, BF16),
        ),
        in_specs=[vmem] * 5 + [hbm],
        out_specs=(vmem, hbm),
        scratch_shapes=[
            pltpu.VMEM((own, count), BF16),
            pltpu.VMEM((lanes // CHUNKS, count), BF16),
            pltpu.VMEM((CHUNKS, spaces * rows, lanes // CHUNKS), BF16),
            pltpu.VMEM((CHUNKS, spaces * rows, lanes // CHUNKS), BF16),
            pltpu.VMEM((lanes // 128, spaces * rows, 128), F32),
            pltpu.VMEM((regions, members, members), BF16),
            pltpu.VMEM((regions, own, members), BF16),
            pltpu.SemaphoreType.DMA((3,)),
            pltpu.SemaphoreType.DMA((3,)),
            pltpu.SemaphoreType.DMA((CHUNKS, spaces)),
            pltpu.SemaphoreType.DMA((CHUNKS, spaces)),
        ],
        compiler_params=pltpu.CompilerParams(
            collective_id=0, has_side_effects=True, vmem_limit_bytes=56 * 2**20
        ),
        name="region_weights",
    )(
        obs_ens, obs_value, obs_weight, obs_region, region_order, background,
    )
    half = own * own_regions
    return pl.pallas_call(
        analysis_kernel,
        out_shape=jax.ShapeDtypeStruct(background.shape, BF16),
        in_specs=[vmem, hbm, hbm],
        out_specs=hbm,
        scratch_shapes=[
            pltpu.VMEM(background.shape, BF16),
            pltpu.VMEM(background.shape, BF16),
            pltpu.VMEM(background.shape, BF16),
            pltpu.VMEM((half + own_regions, 2 * half), BF16),
            pltpu.VMEM((half, 1), F32),
            pltpu.SemaphoreType.DMA((3, width // TILE)),
        ],
        compiler_params=pltpu.CompilerParams(vmem_limit_bytes=60 * 2**20),
        name="analysis",
    )(weights.reshape(half, members), background, other)


def solution(mesh):
    return jax.shard_map(
        functools.partial(shards, mesh.shape["space"]),
        mesh=mesh,
        in_specs=(
            P("member", "space", None),
            P("member", "space"),
            P("space"),
            P("space"),
            P("space"),
            P(),
        ),
        out_specs=P("member", "space", None),
        check_vma=False,
    )
```

```python
import functools

import jax
import jax.numpy as jnp
from jax import lax
from jax.experimental import pallas as pl
from jax.experimental.pallas import tpu as pltpu
from jax.sharding import PartitionSpec as P

NS_ITERS = 4
CAP = 32
PAIR = 2
GROUPS = CAP // PAIR
CHUNKS = 2
TILE = 512
MESH = pl.DeviceIdType.MESH
F32 = jnp.float32
BF16 = jnp.bfloat16


def iota(shape, axis):
    return lax.broadcasted_iota(jnp.int32, shape, axis)


def dot(a, b, dims=((1,), (0,))):
    return lax.dot_general(a, b, (dims, ((), ())), preferred_element_type=F32)


def split(a):
    high = a.astype(BF16)
    return high, (a - high.astype(F32)).astype(BF16)


def dot3(a, b):
    (ah, al), (bh, bl) = a, b
    return dot(ah, bh) + (dot(ah, bl) + dot(al, bh))


def weights_kernel(
    spaces, ens, value, weight, region, region_order, background,
    wall, other_background,
    ens_other, spread, packed, arrived, wide, own_weights, other_weights,
    pair_send, pair_recv, route_send, route_recv,
):
    own, count = ens.shape
    members = 2 * own
    total = region_order.shape[0]
    regions = total // spaces // 2
    rows = regions * PAIR
    m = lax.axis_index("member")
    me = lax.axis_index("space")
    partner = {"member": 1 - m}

    barrier = pltpu.get_barrier_semaphore()
    pl.semaphore_signal(barrier, inc=1, device_id=partner, device_id_type=MESH)

    def greet(step, carry):
        pl.semaphore_signal(
            barrier, inc=1, device_id={"space": lax.rem(me + step, spaces)}, device_id_type=MESH
        )
        return carry

    lax.fori_loop(1, spaces, greet, 0)
    def column(height, per_space, per_region):
        row, col = iota((height, 1), 0), iota((1, total), 1)
        at = row // per_space * (2 * regions) + m * regions + row % per_space // per_region
        held = region_order[...].reshape(1, total).astype(F32)
        picked = jnp.sum(jnp.where(col == at, held, 0.0), axis=1, keepdims=True)
        return picked.astype(jnp.int32)

    order = column(spaces * regions, regions, 1)
    rowkey = column(spaces * rows, rows, PAIR) * PAIR + iota((spaces * rows, 1), 0) % PAIR
    region_row = region[...].reshape(1, count)
    root = jnp.sqrt(weight[...].reshape(1, count).astype(F32))

    pl.semaphore_wait(barrier, spaces)

    def pair_copy(src, dst, index):
        return pltpu.make_async_remote_copy(
            src_ref=src, dst_ref=dst, send_sem=pair_send.at[index], recv_sem=pair_recv.at[index],
            device_id=partner, device_id_type=MESH,
        )

    ens_copy = pair_copy(ens, ens_other, 0)
    ens_copy.start()
    state_copy = pair_copy(background, other_background, 1)
    state_copy.start()

    block = 256
    upper = jnp.where(iota((block, block), 0) < iota((block, block), 1), 1.0, 0.0).astype(BF16)
    offset = jnp.zeros((spaces * regions, 1), F32)
    ranks = []
    for at in range(0, count, block):
        hit = jnp.where(order == region_row[:, at : at + block], 1.0, 0.0)
        earlier = dot(hit.astype(BF16), upper) + offset
        ranks.append(jnp.sum(hit * earlier, axis=0, keepdims=True))
        offset = offset + jnp.sum(hit, axis=1, keepdims=True)
    rank = jnp.concatenate(ranks, axis=1).astype(jnp.int32)
    group = rank // PAIR
    key = region_row * PAIR + rank % PAIR
    picks = jnp.where(rowkey == key, 1.0, 0.0).astype(BF16)

    ens_copy.wait()
    here, there = ens[...].astype(F32), ens_other[...].astype(F32)
    mean = (jnp.sum(here, axis=0, keepdims=True) + jnp.sum(there, axis=0, keepdims=True)) / members
    here = (here - mean) * root
    there = (there - mean) * root
    departure = (value[...].reshape(1, count).astype(F32) - mean) * root
    last = jnp.where(m == 0, there[own - 1 :], here[own - 1 :])
    lift = last / (jnp.sqrt(F32(members)) - 1.0)
    final = iota((own, 1), 0) == own - 1
    here = jnp.where(final & (m == 1), departure, here + lift).astype(BF16)
    there = jnp.where(final & (m == 0), departure, there + lift).astype(BF16)
    def place(index):
        return pl.ds(pl.multiple_of(index * rows, rows), rows)

    def route(chunk, dest, source, landing):
        return pltpu.make_async_remote_copy(
            src_ref=packed.at[chunk, place(dest)], dst_ref=arrived.at[chunk, place(landing)],
            send_sem=route_send.at[chunk, dest], recv_sem=route_recv.at[chunk, source],
            device_id={"space": dest}, device_id_type=MESH,
        )

    span = GROUPS // CHUNKS
    for chunk in range(CHUNKS):
        for g in range(span):
            mask = jnp.where(group == chunk * span + g, 1.0, 0.0).astype(BF16)
            spread[pl.ds(pl.multiple_of(g * members + m * own, own), own), :] = here * mask
            spread[pl.ds(pl.multiple_of(g * members + (1 - m) * own, own), own), :] = there * mask
        packed[chunk] = dot(picks, spread[...], ((1,), (1,))).astype(BF16)

        def send(step, carry):
            route(chunk, lax.rem(me + step, spaces), me, me).start()
            return carry

        lax.fori_loop(1, spaces, send, 0)

    tiles = wide.shape[0] // CHUNKS
    for chunk in range(CHUNKS):

        def receive(step, carry):
            source = lax.rem(me + spaces - step, spaces)
            route(chunk, lax.rem(me + step, spaces), source, source).wait()
            return carry

        arrived[chunk, place(me), :] = packed[chunk, place(me), :]
        lax.fori_loop(1, spaces, receive, 0)
        for j in range(tiles):
            wide[chunk * tiles + j] = arrived[chunk, :, j * 128 : (j + 1) * 128].astype(F32)

    eye = jnp.where(iota((members, members), 0) == iota((members, members), 1), 1.0, 0.0)
    edge = jnp.sqrt(F32(members))
    kept_row, kept_col = iota((1, members), 1) < members - 1, iota((members, 1), 0) < members - 1
    mirror_row = jnp.where(kept_row, 1.0, 1.0 - edge)
    mirror_col = jnp.where(kept_col, 1.0, 1.0 - edge)
    scale = 1.0 / (members - edge)
    systems, projections, norms = [], [], []
    for r in range(regions):
        at = [pl.ds(r * PAIR + k, spaces, stride=rows) for k in range(PAIR)]
        left = [wide[j, at[k], :] for j in range(GROUPS // 2) for k in range(PAIR)]
        anomalies = jnp.concatenate(left, axis=0).astype(BF16)
        gram = dot(anomalies, anomalies, ((0,), (0,)))
        gram = gram[:members, :members] + gram[members:, members:]
        projection = jnp.where(kept_row, gram[members - 1 :], 0.0)
        gram = jnp.where(kept_row & kept_col, gram, 0.0)
        reflected = jnp.sum(projection, axis=1, keepdims=True) * scale
        projections.append(projection - reflected * mirror_row)
        gram = gram - mirror_col * (jnp.sum(gram, axis=0, keepdims=True) * scale)
        gram = gram - (jnp.sum(gram, axis=1, keepdims=True) * scale) * mirror_row
        system = (members - 1.0) * eye + gram
        norm = jnp.sum(jnp.sum(system * system, axis=0, keepdims=True), axis=1, keepdims=True)
        norm = jnp.sqrt(norm)
        norms.append(norm)
        systems.append(system / norm)

    direct = systems
    direct_parts = [split(a) for a in direct]
    correction = [1.5 * eye - 0.5 * a for a in direct]
    inverse = correction
    inverse_parts = [split(a) for a in inverse]
    direct = [dot3(a, c) for a, c in zip(direct_parts, inverse_parts)]
    for iteration in range(1, NS_ITERS):
        direct_parts = [split(a) for a in direct]
        correction = [1.5 * eye - 0.5 * dot3(b, a) for a, b in zip(direct_parts, inverse_parts)]
        correction_parts = [split(a) for a in correction]
        inverse = [dot3(c, b) for c, b in zip(correction_parts, inverse_parts)]
        if iteration < NS_ITERS - 1:
            direct = [dot3(a, c) for a, c in zip(direct_parts, correction_parts)]
            inverse_parts = [split(a) for a in inverse]

    for r in range(regions):
        root_part, norm = inverse[r], norms[r]
        inner = jnp.sum(root_part * projections[r], axis=1, keepdims=True)
        shift = jnp.sum(root_part * inner, axis=0, keepdims=True) / norm
        own_weights[r] = (jnp.sqrt((members - 1.0) / norm) * root_part + shift).astype(BF16)

    mine = pl.ds(pl.multiple_of(m * own, own), own)
    theirs = pl.ds(pl.multiple_of((1 - m) * own, own), own)
    weight_copy = pair_copy(own_weights.at[:, theirs, :], other_weights, 2)
    weight_copy.start()
    wall[m] = own_weights[:, mine, :]
    weight_copy.wait()
    wall[1 - m] = other_weights[...]
    state_copy.wait()


def analysis_kernel(
    weights, here_any, there_any, out_any, here, there, out, wide, retained, sems
):
    own, regions, width = here.shape
    members = 2 * own
    half = own * regions
    tile = TILE
    m = lax.axis_index("member")
    steps = [pl.ds(at, tile) for at in range(0, width, tile)]

    def copy(kind, index):
        source, target = ((here_any, here), (there_any, there), (out, out_any))[kind]
        cut = steps[index]
        return pltpu.make_async_copy(
            source.at[:, :, cut], target.at[:, :, cut], sems.at[kind, index]
        )

    for index in range(len(steps)):
        copy(0, index).start()
        copy(1, index).start()

    row = iota((half, 1), 0)
    region = row % regions
    order = jnp.where(iota((1, half), 1) == region * own + row // regions, 1.0, 0.0)
    order = order.astype(BF16)
    columns = dot(order, weights[...])
    retained[...] = 1.0 - jnp.sum(columns, axis=1, keepdims=True)
    c = iota((1, 2 * half), 1)
    member, lane_region = (c // regions + m * own) % members, c % regions
    copies = jnp.where(member == iota((members, 1), 0), 1.0, 0.0).astype(BF16)
    full = dot(columns.astype(BF16), copies)
    wide[:half] = jnp.where(region == lane_region, full, 0.0).astype(BF16)
    same = iota((regions, 1), 0) == lane_region
    wide[half:] = jnp.where(same, 1.0 / members, 0.0).astype(BF16)

    for index, cut in enumerate(steps):
        copy(0, index).wait()
        copy(1, index).wait()
        total = dot(wide[:, :half], here[:, :, cut].reshape(half, tile))
        total += dot(wide[:, half:], there[:, :, cut].reshape(half, tile))
        combined = total[:half].reshape(own, regions, tile)
        share = retained[...].reshape(own, regions, 1)
        out[:, :, cut] = (combined + share * total[half:][None]).astype(BF16)
        copy(2, index).start()
    for index in range(len(steps)):
        copy(2, index).wait()


def shards(spaces, background, obs_ens, obs_value, obs_weight, obs_region, region_order):
    own, own_regions, width = background.shape
    count = obs_ens.shape[1]
    regions = own_regions // 2
    members = 2 * own
    rows = regions * PAIR
    lanes = GROUPS * members
    vmem = pl.BlockSpec(memory_space=pltpu.VMEM)
    hbm = pl.BlockSpec(memory_space=pl.ANY)
    weights, other = pl.pallas_call(
        functools.partial(weights_kernel, spaces),
        out_shape=(
            jax.ShapeDtypeStruct((2, regions, own, members), BF16),
            jax.ShapeDtypeStruct(background.shape, BF16),
        ),
        in_specs=[vmem] * 5 + [hbm],
        out_specs=(vmem, hbm),
        scratch_shapes=[
            pltpu.VMEM((own, count), BF16),
            pltpu.VMEM((lanes // CHUNKS, count), BF16),
            pltpu.VMEM((CHUNKS, spaces * rows, lanes // CHUNKS), BF16),
            pltpu.VMEM((CHUNKS, spaces * rows, lanes // CHUNKS), BF16),
            pltpu.VMEM((lanes // 128, spaces * rows, 128), F32),
            pltpu.VMEM((regions, members, members), BF16),
            pltpu.VMEM((regions, own, members), BF16),
            pltpu.SemaphoreType.DMA((3,)),
            pltpu.SemaphoreType.DMA((3,)),
            pltpu.SemaphoreType.DMA((CHUNKS, spaces)),
            pltpu.SemaphoreType.DMA((CHUNKS, spaces)),
        ],
        compiler_params=pltpu.CompilerParams(
            collective_id=0, has_side_effects=True, vmem_limit_bytes=56 * 2**20
        ),
        name="region_weights",
    )(
        obs_ens, obs_value, obs_weight, obs_region, region_order, background,
    )
    half = own * own_regions
    return pl.pallas_call(
        analysis_kernel,
        out_shape=jax.ShapeDtypeStruct(background.shape, BF16),
        in_specs=[vmem, hbm, hbm],
        out_specs=hbm,
        scratch_shapes=[
            pltpu.VMEM(background.shape, BF16),
            pltpu.VMEM(background.shape, BF16),
            pltpu.VMEM(background.shape, BF16),
            pltpu.VMEM((half + own_regions, 2 * half), BF16),
            pltpu.VMEM((half, 1), F32),
            pltpu.SemaphoreType.DMA((3, width // TILE)),
        ],
        compiler_params=pltpu.CompilerParams(vmem_limit_bytes=60 * 2**20),
        name="analysis",
    )(weights.reshape(half, members), background, other)


def solution(mesh):
    return jax.shard_map(
        functools.partial(shards, mesh.shape["space"]),
        mesh=mesh,
        in_specs=(
            P("member", "space", None),
            P("member", "space"),
            P("space"),
            P("space"),
            P("space"),
            P(),
        ),
        out_specs=P("member", "space", None),
        check_vma=False,
    )
```
